32 devices in a mesh: branch: 2 (over core), seq: 8 (over z, y), mp: 2 (over x).
Axes of the slice: x: 2, y: 2, z: 4, core: 2. Of those that a mesh axis runs over, the one named last changes fastest.
Arguments:
- tokens: bfloat16 [2048, 4096], P('seq', 'mp'), may hold values from -6 to 6
- light_in: bfloat16 [4096, 2048], P(None, ('branch', 'mp')), may hold values from -0.09375 to 0.09375
- light_out: bfloat16 [2048, 4096], P(('branch', 'mp')), may hold values from -0.1875 to 0.1875
- heavy_in: bfloat16 [4096, 16384], P(None, ('branch', 'seq', 'mp')), may hold values from -0.09375 to 0.09375
- heavy_out: bfloat16 [16384, 4096], P(('branch', 'seq', 'mp')), may hold values from -0.09375 to 0.09375
- route_index: int32 [8, 32], P('seq'), may hold values from 0 to 255, as said below
- route_count: int32 [8], P('seq'), may hold values from 1 to 32, as said below
- route_gate: float32 [8, 32], P('seq'), may hold values from 0.25 to 2
- cotangent: bfloat16 [2048, 4096], P('seq', 'mp'), may hold values from -6 to 6
Outputs:
- mixed: bfloat16 [2048, 4096], P('seq', ('branch', 'mp'))
- grad_heavy_in: bfloat16 [4096, 16384], P(None, ('branch', 'seq', 'mp'))
- grad_heavy_out: bfloat16 [16384, 4096], P(('branch', 'seq', 'mp'))
The draws below stay inside these ranges and needn't reach their ends.
Inputs may be any that keep to these rules, and one draw needn't show every extreme that they name: `route_index`: each row holds 32 distinct positions of its shard. The first route_count[s] slots of shard s are live; some shard has all 32 slots live.
All inputs are finite; a program needn't handle non-finite values.
Results may differ from the reference program's by a relative error of at most 0.008.
Values may be sent and summed in bfloat16 or wider, within the bound.
A program may use at most 128 MiB of HBM per device.

```python
import math
import jax
import jax.numpy as jnp

D = 4096
FFL = 2048
FFH = 16384
TOK_DEV = 256
CAP = 32
TOKENS = 2048
N_SEQ = 8


def draw_route_index(key, part):
    shards = TOKENS // TOK_DEV
    keys = jax.random.split(jax.random.fold_in(key, 11), shards)

    def one_shard(shard_key):
        return jax.random.permutation(shard_key, TOK_DEV)[:CAP]
    return jax.vmap(one_shard)(keys).astype(jnp.int32)


def draw_route_count(key, part):
    shards = TOKENS // TOK_DEV
    lowest = max(CAP // 3, 1)
    counts = jax.random.randint(jax.random.fold_in(key, 21), (shards,), lowest, CAP + 1)
    filled = jax.random.randint(jax.random.fold_in(key, 22), (), 0, shards)
    counts = jnp.where(jnp.arange(shards) == filled, CAP, counts)
    return counts.astype(jnp.int32)


def strengthened(array, rng, source, target, parts, factor):
    def block_of(axis_at):
        return (jnp.arange(array.shape[axis_at]) // (array.shape[axis_at] // parts)).reshape((-1,) + (1,) * (array.ndim - 1 - axis_at))

    first = jax.random.permutation(rng, parts)[block_of(target)]
    second = (block_of(target) + parts // 2) % parts
    return jnp.where((block_of(source) == first) | (block_of(source) == second), factor * array, array)


def levels(rng, dims, pieces, smallest, largest):
    level = 1.0
    for axis_at, blocks in pieces:
        draws = jax.random.uniform(jax.random.fold_in(jax.random.fold_in(rng, 6), axis_at), (blocks,), jnp.float32, smallest / len(pieces), largest / len(pieces))
        level = level * jnp.repeat(jnp.exp(draws), dims[axis_at] // blocks).reshape((-1,) + (1,) * (len(dims) - 1 - axis_at))
    return level


def gaussian(own_key, dims, width, most, cuts=(), kind=jnp.bfloat16):
    result = width * jax.random.normal(own_key, dims, jnp.float32)
    if cuts:
        result = result * levels(own_key, dims, cuts, -0.22, 0.18)
    return jnp.clip(result, -most, most).astype(kind)


def gaussian_with(key, shape, spread, bound, cuts, heavy, kind=jnp.bfloat16):
    values = spread * jax.random.normal(key, shape, jnp.float32)
    if cuts:
        values = values * levels(key, shape, cuts, -0.22, 0.18)
    return jnp.clip(strengthened(values, jax.random.fold_in(key, 3), *heavy), -bound, bound).astype(kind)


def setup_inputs(seed: int = 0) -> dict:
    seeds = jax.random.split(jax.random.key(seed), 10)
    tokens = gaussian(seeds[0], (TOKENS, D), 1.0, 6.0, ((0, 8), (1, 2)))
    light_in = gaussian(seeds[1], (D, FFL), D ** -0.5, 0.09375, ((1, 4),))
    light_out = gaussian_with(seeds[2], (FFL, D), FFL ** -0.5, 0.1875, ((0, 4),), (0, 1, 4, 2.0))
    heavy_in = gaussian(seeds[3], (D, FFH), D ** -0.5, 0.09375, ((1, 32),))
    heavy_out = gaussian_with(seeds[4], (FFH, D), FFH ** -0.5, 0.09375, ((0, 32),), (0, 1, 32, 2.75))
    route_index = draw_route_index(jax.random.fold_in(seeds[9], 71), 0)
    route_count = draw_route_count(jax.random.fold_in(seeds[9], 71), 0)
    route_gate = jnp.clip(jnp.exp(math.log(2.0) - 2.0794415 * jax.random.uniform(seeds[7], (N_SEQ, CAP), jnp.float32) ** levels(seeds[7], (N_SEQ, CAP), ((0, 8),), -0.2, 0.2)), 0.25, 2.0)
    cotangent = gaussian(seeds[8], (TOKENS, D), 1.0, 6.0, ((0, 8), (1, 2)))
    return dict(tokens=tokens, light_in=light_in, light_out=light_out, heavy_in=heavy_in, heavy_out=heavy_out, route_index=route_index, route_count=route_count, route_gate=route_gate, cotangent=cotangent)


root_coef = 0.7978845608
cubic_coef = 0.044715


def gelu_tanh(values):
    inner = root_coef * (values + cubic_coef * values * values * values)
    return 0.5 * values * (1.0 + jnp.tanh(inner))


def gelu_slope(values):
    tangent = jnp.tanh(root_coef * (values + cubic_coef * values * values * values))
    return 0.5 * (1.0 + tangent) + 0.5 * values * (1.0 - tangent * tangent) * root_coef * (1.0 + 3.0 * cubic_coef * values * values)


def reference(tokens, light_in, light_out, heavy_in, heavy_out, route_index, route_count, route_gate, cotangent):
    light_hidden = gelu_tanh(jnp.dot(tokens, light_in, preferred_element_type=jnp.float32)).astype(jnp.bfloat16)
    light_y = jnp.dot(light_hidden, light_out, preferred_element_type=jnp.float32)
    shard_base = (jnp.arange(N_SEQ, dtype=jnp.int32) * TOK_DEV)[:, None]
    picked_rows = (route_index.astype(jnp.int32) + shard_base).reshape(-1)
    live_slots = jnp.arange(CAP, dtype=jnp.int32)[None, :] < route_count[:, None]
    row_scale = jnp.where(live_slots, route_gate, jnp.zeros_like(route_gate)).reshape(-1)
    picked = tokens[picked_rows]
    pre_act = jnp.dot(picked, heavy_in, preferred_element_type=jnp.float32)
    heavy_hidden = gelu_tanh(pre_act).astype(jnp.bfloat16)
    heavy_y = jnp.dot(heavy_hidden, heavy_out, preferred_element_type=jnp.float32) * row_scale[:, None]
    mixed = light_y.at[picked_rows].add(heavy_y).astype(jnp.bfloat16)
    back_rows = (cotangent[picked_rows].astype(jnp.float32) * row_scale[:, None]).astype(jnp.bfloat16)
    grad_heavy_out = jnp.dot(heavy_hidden.T, back_rows, preferred_element_type=jnp.float32).astype(jnp.bfloat16)
    slope = (jnp.dot(back_rows, heavy_out.T, preferred_element_type=jnp.float32) * gelu_slope(pre_act)).astype(jnp.bfloat16)
    grad_heavy_in = jnp.dot(picked.T, slope, preferred_element_type=jnp.float32).astype(jnp.bfloat16)
    return mixed, grad_heavy_in, grad_heavy_out
```

```python
import functools

import jax
import jax.numpy as jnp
from jax import lax
from jax.experimental import pallas as pl
from jax.experimental.pallas import tpu as pltpu
from jax.sharding import PartitionSpec as P

root_coef = 0.7978845608
cubic_coef = 0.044715
MESH = pl.DeviceIdType.MESH
F32 = jnp.float32
BF16 = jnp.bfloat16


def gelu_both(values):
    square = values * values
    tangent = jnp.tanh(root_coef * (values + cubic_coef * square * values))
    half = 0.5 * (1.0 + tangent)
    slope = half + 0.5 * values * (1.0 - tangent * tangent) * root_coef * (
        1.0 + 3.0 * cubic_coef * square
    )
    return values * half, slope


def gelu_tanh(values):
    return gelu_both(values)[0]


def over_rows(left, right):
    return lax.dot_general(left, right, (((0,), (0,)), ((), ())), preferred_element_type=F32)


def over_cols(left, right):
    return lax.dot_general(left, right, (((1,), (1,)), ((), ())), preferred_element_type=F32)


def dot(left, right):
    return jnp.dot(left, right, preferred_element_type=F32)


def tile_of(size, most):
    tile = min(size, most)
    while size % tile:
        tile //= 2
    return tile


def kernel(
    n_seq,
    sizes,
    tokens,
    light_in,
    light_out,
    heavy_in,
    heavy_out,
    index,
    count,
    gate,
    cotangent,
    mixed,
    rows_out,
    hidden,
    slope,
    whole,
    cot,
    w_lin,
    w_lout,
    w_hin,
    w_hout,
    rows_all,
    l_hidden,
    l_own,
    l_send,
    l_recv,
    l_xsend,
    l_xrecv,
    h_slope,
    h_own,
    h_send,
    h_recv,
    y_send,
    y_recv,
    z_send,
    z_recv,
    x_send,
    x_recv,
    local_sem,
    send_sem,
    recv_sem,
):
    tok, half_d, ffl, ffh, cap = sizes
    width = 2 * half_d
    out_w = width // 4
    n_hi = n_seq // 2
    part = cap // 2
    total_rows = n_seq * cap
    b = lax.axis_index("branch")
    s = lax.axis_index("seq")
    m = lax.axis_index("mp")
    hi, lo = s // 2, s % 2
    sibling = {"branch": 1 - b}
    across = {"mp": 1 - m}
    beside = {"seq": hi * 2 + (1 - lo)}

    def hi_plus(d):
        return lax.rem(hi + d, n_hi)

    def hi_less(d):
        return lax.rem(hi + (n_hi - d), n_hi)

    local = []

    def load(src, dst):
        copy = pltpu.make_async_copy(src, dst, local_sem.at[len(local)])
        copy.start()
        local.append(copy)
        return copy

    own_cols = pl.ds(pl.multiple_of(m * half_d, half_d), half_d)
    load_tok = load(tokens, whole.at[:, own_cols])
    load_cot = load(cotangent, cot)
    load_lin = load(light_in, w_lin)
    load_lout = load(light_out, w_lout)
    load_hin = load(heavy_in, w_hin)
    load_hout = load(heavy_out, w_hout)

    barrier = pltpu.get_barrier_semaphore()
    peers = [sibling, across, beside] + [{"seq": hi_plus(d) * 2 + lo} for d in range(1, n_hi)]
    for peer in peers:
        pl.semaphore_signal(barrier, inc=1, device_id=peer, device_id_type=MESH)

    names = index[...].astype(F32)
    live = lax.broadcasted_iota(jnp.int32, (1, cap), 1) < count[0]
    scale_row = jnp.where(live, gate[...], 0.0)

    def column_of(row, first, rows):
        at = lax.broadcasted_iota(jnp.int32, (rows, cap), 0) + first
        to = lax.broadcasted_iota(jnp.int32, (rows, cap), 1)
        spread = jnp.where(at == to, jnp.broadcast_to(row, (rows, cap)), 0.0)
        return jnp.sum(spread, axis=1, keepdims=True)

    names_col = column_of(names, b * part, part)
    scale_part = column_of(scale_row, b * part, part)
    choose = jnp.where(
        lax.broadcasted_iota(jnp.int32, (part, tok), 1).astype(F32) == names_col, 1.0, 0.0
    ).astype(BF16)

    def rows_of(hi_at, lo_at, half):
        return pl.ds(pl.multiple_of((hi_at * 2 + lo_at) * cap + half * part, part), part)

    mine = rows_of(hi, lo, b)
    load_tok.wait()
    rows_all[0, mine, own_cols] = dot(choose, whole[:, own_cols]).astype(BF16)
    load_cot.wait()
    rows_all[1, mine, own_cols] = (dot(choose, cot[...]) * scale_part).astype(BF16)

    pl.semaphore_wait(barrier, len(peers))

    keys = {}
    sends = []

    def key_of(key):
        return keys.setdefault(key, len(keys))

    def send(key, src, dst, device):
        at = key_of(key)
        copy = pltpu.make_async_remote_copy(
            src_ref=src,
            dst_ref=dst,
            send_sem=send_sem.at[at],
            recv_sem=recv_sem.at[at],
            device_id=device,
            device_id_type=MESH,
        )
        copy.start()
        sends.append(copy)

    def arrive(key, dst, device):
        at = key_of(key)
        pltpu.make_async_remote_copy(
            src_ref=dst,
            dst_ref=dst,
            send_sem=send_sem.at[at],
            recv_sem=recv_sem.at[at],
            device_id=device,
            device_id_type=MESH,
        ).wait_recv()

    other_cols = pl.ds(pl.multiple_of((1 - m) * half_d, half_d), half_d)
    for k in range(2):
        view = rows_all.at[k, mine, own_cols]
        send(("x", k), view, view, across)
    tok_half = tok // 2
    my_tok = pl.ds(pl.multiple_of(b * tok_half, tok_half), tok_half)
    its_tok = pl.ds(pl.multiple_of((1 - b) * tok_half, tok_half), tok_half)
    send("tok", tokens.at[my_tok], whole.at[my_tok, own_cols], across)

    for k in range(2):
        arrive(("x", k), rows_all.at[k, mine, other_cols], across)
        view = rows_all.at[k, mine]
        for d in range(1, n_hi):
            send(("z", k, d), view, view, {"seq": hi_plus(d) * 2 + lo})
        send(("y", k, 0), view, view, beside)
        send(("s", k, 0, 0), view, view, sibling)

    def from_z(k):
        for d in range(1, n_hi):
            view = rows_all.at[k, rows_of(hi_less(d), lo, b)]
            arrive(("z", k, d), view, {"seq": hi_less(d) * 2 + lo})
            send(("y", k, d), view, view, beside)
            send(("s", k, 0, d), view, view, sibling)

    def from_y(k):
        for d in range(n_hi):
            view = rows_all.at[k, rows_of(hi_less(d), 1 - lo, b)]
            arrive(("y", k, d), view, beside)
            send(("s", k, 1, d), view, view, sibling)

    def from_sibling(k):
        for side in range(2):
            for d in range(n_hi):
                at = lo if side == 0 else 1 - lo
                view = rows_all.at[k, rows_of(hi_less(d), at, 1 - b)]
                arrive(("s", k, side, d), view, sibling)

    from_z(0)
    arrive("tok", whole.at[my_tok, other_cols], across)
    view = whole.at[my_tok, other_cols]
    send("tok2", view, view, sibling)
    from_y(0)
    from_z(1)

    arrive("tok2", whole.at[its_tok, other_cols], sibling)
    load_lin.wait()
    t_l = tile_of(ffl, 256)

    @pl.loop(0, ffl // t_l)
    def _(i):
        cols = pl.ds(pl.multiple_of(i * t_l, t_l), t_l)
        l_hidden[:, cols] = gelu_tanh(dot(whole[...], w_lin[:, cols])).astype(BF16)

    load_lout.wait()
    t_o = tile_of(half_d, 512)

    @pl.loop(0, half_d // t_o)
    def _(i):
        cols = pl.ds(pl.multiple_of(i * t_o, t_o), t_o)
        there = pl.ds(pl.multiple_of((1 - b) * half_d + i * t_o, t_o), t_o)
        l_send[:, cols] = dot(l_hidden[...], w_lout[:, there]).astype(BF16)

    send("l", l_send, l_recv, sibling)

    @pl.loop(0, half_d // t_o)
    def _(i):
        cols = pl.ds(pl.multiple_of(i * t_o, t_o), t_o)
        here = pl.ds(pl.multiple_of(b * half_d + i * t_o, t_o), t_o)
        l_own[:, cols] = dot(l_hidden[...], w_lout[:, here])

    from_sibling(0)
    load_hin.wait()
    t_h = tile_of(ffh, 256)
    t_r = tile_of(total_rows, 256)

    @pl.loop(0, total_rows // t_r)
    def _(j):
        rows = pl.ds(pl.multiple_of(j * t_r, t_r), t_r)

        @pl.loop(0, ffh // t_h)
        def _(i):
            cols = pl.ds(pl.multiple_of(i * t_h, t_h), t_h)
            value, rate = gelu_both(dot(rows_all[0, rows, :], w_hin[:, cols]))
            hidden[rows, cols] = value.astype(BF16)
            h_slope[rows, cols] = rate

    load_hout.wait()

    @pl.loop(0, total_rows // t_r)
    def _(j):
        rows = pl.ds(pl.multiple_of(j * t_r, t_r), t_r)

        @pl.loop(0, half_d // t_o)
        def _(i):
            cols = pl.ds(pl.multiple_of(i * t_o, t_o), t_o)
            there = pl.ds(pl.multiple_of((1 - b) * half_d + i * t_o, t_o), t_o)
            h_send[rows, cols] = dot(hidden[rows, :], w_hout[:, there]).astype(BF16)

    send("h", h_send, h_recv, sibling)

    @pl.loop(0, total_rows // t_r)
    def _(j):
        rows = pl.ds(pl.multiple_of(j * t_r, t_r), t_r)

        @pl.loop(0, half_d // t_o)
        def _(i):
            cols = pl.ds(pl.multiple_of(i * t_o, t_o), t_o)
            here = pl.ds(pl.multiple_of(b * half_d + i * t_o, t_o), t_o)
            h_own[rows, cols] = dot(hidden[rows, :], w_hout[:, here])

    arrive("h", h_recv, sibling)

    def shard_rows(hi_at, lo_at):
        return pl.ds(pl.multiple_of((hi_at * 2 + lo_at) * cap, cap), cap)

    for d in range(n_hi):
        at = hi_plus((d + 1) % n_hi)
        rows = shard_rows(at, 1 - lo)
        y_send[d] = (h_own[rows, :] + h_recv[rows, :].astype(F32)).astype(BF16)
        send(("hy", d), y_send.at[d], y_recv.at[d], beside)

    my_out = pl.ds(pl.multiple_of(m * out_w, out_w), out_w)
    its_out = pl.ds(pl.multiple_of((1 - m) * out_w, out_w), out_w)
    arrive("l", l_recv, sibling)
    l_xsend[...] = (l_own[:, its_out] + l_recv[:, its_out].astype(F32)).astype(BF16)
    send("lx", l_xsend, l_xrecv, across)

    from_y(1)
    kept = None
    for d in range(n_hi):
        step = (d + 1) % n_hi
        rows = shard_rows(hi_plus(step), lo)
        arrive(("hy", d), y_recv.at[d], beside)
        total = h_own[rows, :] + h_recv[rows, :].astype(F32) + y_recv[d].astype(F32)
        if step:
            z_send[step - 1] = total.astype(BF16)
            send(
                ("hz", step),
                z_send.at[step - 1],
                z_recv.at[step - 1],
                {"seq": hi_plus(step) * 2 + lo},
            )
        else:
            h_own[rows, :] = total

    from_sibling(1)
    store_rows = pltpu.make_async_copy(rows_all, rows_out, local_sem.at[len(local)])
    store_rows.start()

    @pl.loop(0, total_rows // t_r)
    def _(j):
        rows = pl.ds(pl.multiple_of(j * t_r, t_r), t_r)

        @pl.loop(0, ffh // t_h)
        def _(i):
            cols = pl.ds(pl.multiple_of(i * t_h, t_h), t_h)
            back = over_cols(rows_all[1, rows, :], w_hout[cols, :])
            slope[rows, cols] = (back * h_slope[rows, cols]).astype(BF16)

    home = shard_rows(hi, lo)
    for d in range(1, n_hi):
        arrive(("hz", d), z_recv.at[d - 1], {"seq": hi_less(d) * 2 + lo})
        h_own[home, :] = h_own[home, :] + z_recv[d - 1].astype(F32)
    x_send[...] = h_own[home, its_out].astype(BF16)
    send("hx", x_send, x_recv, across)
    arrive("lx", l_xrecv, across)
    arrive("hx", x_recv, across)

    share = (h_own[home, my_out] + x_recv[...].astype(F32)) * column_of(scale_row, 0, cap)
    coarse = share.astype(BF16)
    fine = (share - coarse.astype(F32)).astype(BF16)
    place = jnp.where(
        lax.broadcasted_iota(jnp.int32, (tok, cap), 0).astype(F32) == names, 1.0, 0.0
    ).astype(BF16)
    light = l_own[:, my_out] + l_recv[:, my_out].astype(F32) + l_xrecv[...].astype(F32)
    mixed[...] = (light + dot(place, coarse) + dot(place, fine)).astype(BF16)

    store_rows.wait()
    for copy in sends:
        copy.wait_send()


def per_device(
    n_seq,
    tokens,
    light_in,
    light_out,
    heavy_in,
    heavy_out,
    route_index,
    route_count,
    route_gate,
    cotangent,
):
    tok, half_d = tokens.shape
    width = 2 * half_d
    ffl = light_in.shape[1]
    ffh = heavy_in.shape[1]
    cap = route_index.shape[1]
    n_hi = n_seq // 2
    total_rows = n_seq * cap
    out_w = width // 4
    n_sem = 8 + 10 * n_hi
    vmem = pl.BlockSpec(memory_space=pltpu.VMEM)
    smem = pl.BlockSpec(memory_space=pltpu.SMEM)
    hbm = pl.BlockSpec(memory_space=pl.ANY)
    mixed, rows, hidden, slope = pl.pallas_call(
        functools.partial(kernel, n_seq, (tok, half_d, ffl, ffh, cap)),
        out_shape=(
            jax.ShapeDtypeStruct((tok, out_w), BF16),
            jax.ShapeDtypeStruct((2, total_rows, width), BF16),
            jax.ShapeDtypeStruct((total_rows, ffh), BF16),
            jax.ShapeDtypeStruct((total_rows, ffh), BF16),
        ),
        in_specs=[hbm, hbm, hbm, hbm, hbm, vmem, smem, vmem, hbm],
        out_specs=(vmem, hbm, vmem, vmem),
        scratch_shapes=[
            pltpu.VMEM((tok, width), BF16),
            pltpu.VMEM((tok, half_d), BF16),
            pltpu.VMEM(light_in.shape, BF16),
            pltpu.VMEM(light_out.shape, BF16),
            pltpu.VMEM(heavy_in.shape, BF16),
            pltpu.VMEM(heavy_out.shape, BF16),
            pltpu.VMEM((2, total_rows, width), BF16),
            pltpu.VMEM((tok, ffl), BF16),
            pltpu.VMEM((tok, half_d), F32),
            pltpu.VMEM((tok, half_d), BF16),
            pltpu.VMEM((tok, half_d), BF16),
            pltpu.VMEM((tok, out_w), BF16),
            pltpu.VMEM((tok, out_w), BF16),
            pltpu.VMEM((total_rows, ffh), F32),
            pltpu.VMEM((total_rows, half_d), F32),
            pltpu.VMEM((total_rows, half_d), BF16),
            pltpu.VMEM((total_rows, half_d), BF16),
            pltpu.VMEM((n_hi, cap, half_d), BF16),
            pltpu.VMEM((n_hi, cap, half_d), BF16),
            pltpu.VMEM((n_hi - 1, cap, half_d), BF16),
            pltpu.VMEM((n_hi - 1, cap, half_d), BF16),
            pltpu.VMEM((cap, out_w), BF16),
            pltpu.VMEM((cap, out_w), BF16),
            pltpu.SemaphoreType.DMA((8,)),
            pltpu.SemaphoreType.DMA((n_sem,)),
            pltpu.SemaphoreType.DMA((n_sem,)),
        ],
        compiler_params=pltpu.CompilerParams(
            collective_id=0, has_side_effects=True, vmem_limit_bytes=60 * 1024 * 1024
        ),
    )(
        tokens,
        light_in,
        light_out,
        heavy_in,
        heavy_out,
        route_index,
        route_count,
        route_gate,
        cotangent,
    )
    grad_out = over_rows(hidden, rows[1]).astype(BF16)
    grad_in = over_rows(rows[0], slope).astype(BF16)
    return mixed, grad_in, grad_out


def solution(mesh):
    in_specs = (
        P("seq", "mp"),
        P(None, ("branch", "mp")),
        P(("branch", "mp"), None),
        P(None, ("branch", "seq", "mp")),
        P(("branch", "seq", "mp"), None),
        P("seq", None),
        P("seq"),
        P("seq", None),
        P("seq", "mp"),
    )
    out_specs = (
        P("seq", ("branch", "mp")),
        P(None, ("branch", "seq", "mp")),
        P(("branch", "seq", "mp"), None),
    )
    return jax.shard_map(
        functools.partial(per_device, mesh.shape["seq"]),
        mesh=mesh,
        in_specs=in_specs,
        out_specs=out_specs,
        check_vma=False,
    )
```

```python
import functools

import jax
import jax.numpy as jnp
from jax import lax
from jax.experimental import pallas as pl
from jax.experimental.pallas import tpu as pltpu
from jax.sharding import PartitionSpec as P

root_coef = 0.7978845608
cubic_coef = 0.044715
MESH = pl.DeviceIdType.MESH
F32 = jnp.float32
BF16 = jnp.bfloat16


def gelu_both(values):
    square = values * values
    tangent = jnp.tanh(root_coef * (values + cubic_coef * square * values))
    half = 0.5 * (1.0 + tangent)
    slope = half + 0.5 * values * (1.0 - tangent * tangent) * root_coef * (
        1.0 + 3.0 * cubic_coef * square
    )
    return values * half, slope


def gelu_tanh(values):
    return gelu_both(values)[0]


def over_rows(left, right):
    return lax.dot_general(left, right, (((0,), (0,)), ((), ())), preferred_element_type=F32)


def over_cols(left, right):
    return lax.dot_general(left, right, (((1,), (1,)), ((), ())), preferred_element_type=F32)


def dot(left, right):
    return jnp.dot(left, right, preferred_element_type=F32)


def tile_of(size, most):
    tile = min(size, most)
    while size % tile:
        tile //= 2
    return tile


def kernel(
    n_seq,
    sizes,
    tokens,
    light_in,
    light_out,
    heavy_in,
    heavy_out,
    index,
    count,
    gate,
    cotangent,
    mixed,
    rows_out,
    hidden,
    slope,
    whole,
    cot,
    w_lin,
    w_lout,
    w_hin,
    w_hout,
    rows_all,
    l_hidden,
    l_own,
    l_send,
    l_recv,
    l_xsend,
    l_xrecv,
    h_slope,
    h_own,
    h_send,
    h_recv,
    y_send,
    y_recv,
    z_send,
    z_recv,
    x_send,
    x_recv,
    local_sem,
    send_sem,
    recv_sem,
):
    tok, half_d, ffl, ffh, cap = sizes
    width = 2 * half_d
    out_w = width // 4
    n_hi = n_seq // 2
    part = cap // 2
    total_rows = n_seq * cap
    b = lax.axis_index("branch")
    s = lax.axis_index("seq")
    m = lax.axis_index("mp")
    hi, lo = s // 2, s % 2
    sibling = {"branch": 1 - b}
    across = {"mp": 1 - m}
    beside = {"seq": hi * 2 + (1 - lo)}

    def hi_plus(d):
        return lax.rem(hi + d, n_hi)

    def hi_less(d):
        return lax.rem(hi + (n_hi - d), n_hi)

    local = []

    def load(src, dst):
        copy = pltpu.make_async_copy(src, dst, local_sem.at[len(local)])
        copy.start()
        local.append(copy)
        return copy

    own_cols = pl.ds(pl.multiple_of(m * half_d, half_d), half_d)
    load_tok = load(tokens, whole.at[:, own_cols])
    load_cot = load(cotangent, cot)
    load_lin = load(light_in, w_lin)
    load_lout = load(light_out, w_lout)
    load_hin = load(heavy_in, w_hin)
    load_hout = load(heavy_out, w_hout)

    barrier = pltpu.get_barrier_semaphore()
    peers = [sibling, across, beside] + [{"seq": hi_plus(d) * 2 + lo} for d in range(1, n_hi)]
    for peer in peers:
        pl.semaphore_signal(barrier, inc=1, device_id=peer, device_id_type=MESH)

    names = index[...].astype(F32)
    live = lax.broadcasted_iota(jnp.int32, (1, cap), 1) < count[0]
    scale_row = jnp.where(live, gate[...], 0.0)

    def column_of(row, first, rows):
        at = lax.broadcasted_iota(jnp.int32, (rows, cap), 0) + first
        to = lax.broadcasted_iota(jnp.int32, (rows, cap), 1)
        spread = jnp.where(at == to, jnp.broadcast_to(row, (rows, cap)), 0.0)
        return jnp.sum(spread, axis=1, keepdims=True)

    names_col = column_of(names, b * part, part)
    scale_part = column_of(scale_row, b * part, part)
    choose = jnp.where(
        lax.broadcasted_iota(jnp.int32, (part, tok), 1).astype(F32) == names_col, 1.0, 0.0
    ).astype(BF16)

    def rows_of(hi_at, lo_at, half):
        return pl.ds(pl.multiple_of((hi_at * 2 + lo_at) * cap + half * part, part), part)

    mine = rows_of(hi, lo, b)
    load_tok.wait()
    rows_all[0, mine, own_cols] = dot(choose, whole[:, own_cols]).astype(BF16)
    load_cot.wait()
    rows_all[1, mine, own_cols] = (dot(choose, cot[...]) * scale_part).astype(BF16)

    pl.semaphore_wait(barrier, len(peers))

    keys = {}
    sends = []

    def key_of(key):
        return keys.setdefault(key, len(keys))

    def send(key, src, dst, device):
        at = key_of(key)
        copy = pltpu.make_async_remote_copy(
            src_ref=src,
            dst_ref=dst,
            send_sem=send_sem.at[at],
            recv_sem=recv_sem.at[at],
            device_id=device,
            device_id_type=MESH,
        )
        copy.start()
        sends.append(copy)

    def arrive(key, dst, device):
        at = key_of(key)
        pltpu.make_async_remote_copy(
            src_ref=dst,
            dst_ref=dst,
            send_sem=send_sem.at[at],
            recv_sem=recv_sem.at[at],
            device_id=device,
            device_id_type=MESH,
        ).wait_recv()

    other_cols = pl.ds(pl.multiple_of((1 - m) * half_d, half_d), half_d)
    for k in range(2):
        view = rows_all.at[k, mine, own_cols]
        send(("x", k), view, view, across)
    tok_half = tok // 2
    my_tok = pl.ds(pl.multiple_of(b * tok_half, tok_half), tok_half)
    its_tok = pl.ds(pl.multiple_of((1 - b) * tok_half, tok_half), tok_half)
    send("tok", tokens.at[my_tok], whole.at[my_tok, own_cols], across)

    def begin(k):
        arrive(("x", k), rows_all.at[k, mine, other_cols], across)
        view = rows_all.at[k, mine]
        for d in range(1, n_hi):
            send(("z", k, d), view, view, {"seq": hi_plus(d) * 2 + lo})
        send(("y", k, 0), view, view, beside)
        send(("s", k, 0, 0), view, view, sibling)

    def from_z(k):
        for d in range(1, n_hi):
            view = rows_all.at[k, rows_of(hi_less(d), lo, b)]
            arrive(("z", k, d), view, {"seq": hi_less(d) * 2 + lo})
            send(("y", k, d), view, view, beside)
            send(("s", k, 0, d), view, view, sibling)

    def from_y(k):
        for d in range(n_hi):
            view = rows_all.at[k, rows_of(hi_less(d), 1 - lo, b)]
            arrive(("y", k, d), view, beside)
            send(("s", k, 1, d), view, view, sibling)

    def from_sibling(k):
        for side in range(2):
            for d in range(n_hi):
                at = lo if side == 0 else 1 - lo
                view = rows_all.at[k, rows_of(hi_less(d), at, 1 - b)]
                arrive(("s", k, side, d), view, sibling)

    begin(0)
    from_z(0)
    begin(1)
    arrive("tok", whole.at[my_tok, other_cols], across)
    view = whole.at[my_tok, other_cols]
    send("tok2", view, view, sibling)

    arrive("tok2", whole.at[its_tok, other_cols], sibling)
    load_lin.wait()
    t_l = tile_of(ffl, 256)

    @pl.loop(0, ffl // t_l)
    def _(i):
        cols = pl.ds(pl.multiple_of(i * t_l, t_l), t_l)
        l_hidden[:, cols] = gelu_tanh(dot(whole[...], w_lin[:, cols])).astype(BF16)

    load_lout.wait()
    t_o = tile_of(half_d, 512)

    @pl.loop(0, half_d // t_o)
    def _(i):
        cols = pl.ds(pl.multiple_of(i * t_o, t_o), t_o)
        there = pl.ds(pl.multiple_of((1 - b) * half_d + i * t_o, t_o), t_o)
        l_send[:, cols] = dot(l_hidden[...], w_lout[:, there]).astype(BF16)

    send("l", l_send, l_recv, sibling)
    from_z(1)
    from_y(0)

    @pl.loop(0, half_d // t_o)
    def _(i):
        cols = pl.ds(pl.multiple_of(i * t_o, t_o), t_o)
        here = pl.ds(pl.multiple_of(b * half_d + i * t_o, t_o), t_o)
        l_own[:, cols] = dot(l_hidden[...], w_lout[:, here])

    from_sibling(0)
    load_hin.wait()
    t_h = tile_of(ffh, 256)
    t_r = tile_of(total_rows, 256)

    @pl.loop(0, total_rows // t_r)
    def _(j):
        rows = pl.ds(pl.multiple_of(j * t_r, t_r), t_r)

        @pl.loop(0, ffh // t_h)
        def _(i):
            cols = pl.ds(pl.multiple_of(i * t_h, t_h), t_h)
            value, rate = gelu_both(dot(rows_all[0, rows, :], w_hin[:, cols]))
            hidden[rows, cols] = value.astype(BF16)
            h_slope[rows, cols] = rate

    load_hout.wait()

    @pl.loop(0, total_rows // t_r)
    def _(j):
        rows = pl.ds(pl.multiple_of(j * t_r, t_r), t_r)

        @pl.loop(0, half_d // t_o)
        def _(i):
            cols = pl.ds(pl.multiple_of(i * t_o, t_o), t_o)
            there = pl.ds(pl.multiple_of((1 - b) * half_d + i * t_o, t_o), t_o)
            h_send[rows, cols] = dot(hidden[rows, :], w_hout[:, there]).astype(BF16)

    send("h", h_send, h_recv, sibling)

    @pl.loop(0, total_rows // t_r)
    def _(j):
        rows = pl.ds(pl.multiple_of(j * t_r, t_r), t_r)

        @pl.loop(0, half_d // t_o)
        def _(i):
            cols = pl.ds(pl.multiple_of(i * t_o, t_o), t_o)
            here = pl.ds(pl.multiple_of(b * half_d + i * t_o, t_o), t_o)
            h_own[rows, cols] = dot(hidden[rows, :], w_hout[:, here])

    arrive("h", h_recv, sibling)

    def shard_rows(hi_at, lo_at):
        return pl.ds(pl.multiple_of((hi_at * 2 + lo_at) * cap, cap), cap)

    for d in range(n_hi):
        at = hi_plus((d + 1) % n_hi)
        rows = shard_rows(at, 1 - lo)
        y_send[d] = (h_own[rows, :] + h_recv[rows, :].astype(F32)).astype(BF16)
        send(("hy", d), y_send.at[d], y_recv.at[d], beside)

    my_out = pl.ds(pl.multiple_of(m * out_w, out_w), out_w)
    its_out = pl.ds(pl.multiple_of((1 - m) * out_w, out_w), out_w)
    arrive("l", l_recv, sibling)
    l_xsend[...] = (l_own[:, its_out] + l_recv[:, its_out].astype(F32)).astype(BF16)
    send("lx", l_xsend, l_xrecv, across)

    from_y(1)
    kept = None
    for d in range(n_hi):
        step = (d + 1) % n_hi
        rows = shard_rows(hi_plus(step), lo)
        arrive(("hy", d), y_recv.at[d], beside)
        total = h_own[rows, :] + h_recv[rows, :].astype(F32) + y_recv[d].astype(F32)
        if step:
            z_send[step - 1] = total.astype(BF16)
            send(
                ("hz", step),
                z_send.at[step - 1],
                z_recv.at[step - 1],
                {"seq": hi_plus(step) * 2 + lo},
            )
        else:
            h_own[rows, :] = total

    from_sibling(1)
    store_rows = pltpu.make_async_copy(rows_all, rows_out, local_sem.at[len(local)])
    store_rows.start()

    @pl.loop(0, total_rows // t_r)
    def _(j):
        rows = pl.ds(pl.multiple_of(j * t_r, t_r), t_r)

        @pl.loop(0, ffh // t_h)
        def _(i):
            cols = pl.ds(pl.multiple_of(i * t_h, t_h), t_h)
            back = over_cols(rows_all[1, rows, :], w_hout[cols, :])
            slope[rows, cols] = (back * h_slope[rows, cols]).astype(BF16)

    home = shard_rows(hi, lo)
    for d in range(1, n_hi):
        arrive(("hz", d), z_recv.at[d - 1], {"seq": hi_less(d) * 2 + lo})
        h_own[home, :] = h_own[home, :] + z_recv[d - 1].astype(F32)
    x_send[...] = h_own[home, its_out].astype(BF16)
    send("hx", x_send, x_recv, across)
    arrive("lx", l_xrecv, across)
    arrive("hx", x_recv, across)

    share = (h_own[home, my_out] + x_recv[...].astype(F32)) * column_of(scale_row, 0, cap)
    coarse = share.astype(BF16)
    fine = (share - coarse.astype(F32)).astype(BF16)
    place = jnp.where(
        lax.broadcasted_iota(jnp.int32, (tok, cap), 0).astype(F32) == names, 1.0, 0.0
    ).astype(BF16)
    light = l_own[:, my_out] + l_recv[:, my_out].astype(F32) + l_xrecv[...].astype(F32)
    mixed[...] = (light + dot(place, coarse) + dot(place, fine)).astype(BF16)

    store_rows.wait()
    for copy in sends:
        copy.wait_send()


def grad_kernel(rows, hidden, slope, grad_in, grad_out):
    grad_in[...] = over_rows(rows[0], slope[...]).astype(BF16)
    grad_out[...] = over_rows(hidden[...], rows[1]).astype(BF16)


def per_device(
    n_seq,
    tokens,
    light_in,
    light_out,
    heavy_in,
    heavy_out,
    route_index,
    route_count,
    route_gate,
    cotangent,
):
    tok, half_d = tokens.shape
    width = 2 * half_d
    ffl = light_in.shape[1]
    ffh = heavy_in.shape[1]
    cap = route_index.shape[1]
    n_hi = n_seq // 2
    total_rows = n_seq * cap
    out_w = width // 4
    n_sem = 8 + 10 * n_hi
    vmem = pl.BlockSpec(memory_space=pltpu.VMEM)
    smem = pl.BlockSpec(memory_space=pltpu.SMEM)
    hbm = pl.BlockSpec(memory_space=pl.ANY)
    mixed, rows, hidden, slope = pl.pallas_call(
        functools.partial(kernel, n_seq, (tok, half_d, ffl, ffh, cap)),
        out_shape=(
            jax.ShapeDtypeStruct((tok, out_w), BF16),
            jax.ShapeDtypeStruct((2, total_rows, width), BF16),
            jax.ShapeDtypeStruct((total_rows, ffh), BF16),
            jax.ShapeDtypeStruct((total_rows, ffh), BF16),
        ),
        in_specs=[hbm, hbm, hbm, hbm, hbm, vmem, smem, vmem, hbm],
        out_specs=(vmem, hbm, vmem, vmem),
        scratch_shapes=[
            pltpu.VMEM((tok, width), BF16),
            pltpu.VMEM((tok, half_d), BF16),
            pltpu.VMEM(light_in.shape, BF16),
            pltpu.VMEM(light_out.shape, BF16),
            pltpu.VMEM(heavy_in.shape, BF16),
            pltpu.VMEM(heavy_out.shape, BF16),
            pltpu.VMEM((2, total_rows, width), BF16),
            pltpu.VMEM((tok, ffl), BF16),
            pltpu.VMEM((tok, half_d), F32),
            pltpu.VMEM((tok, half_d), BF16),
            pltpu.VMEM((tok, half_d), BF16),
            pltpu.VMEM((tok, out_w), BF16),
            pltpu.VMEM((tok, out_w), BF16),
            pltpu.VMEM((total_rows, ffh), F32),
            pltpu.VMEM((total_rows, half_d), F32),
            pltpu.VMEM((total_rows, half_d), BF16),
            pltpu.VMEM((total_rows, half_d), BF16),
            pltpu.VMEM((n_hi, cap, half_d), BF16),
            pltpu.VMEM((n_hi, cap, half_d), BF16),
            pltpu.VMEM((n_hi - 1, cap, half_d), BF16),
            pltpu.VMEM((n_hi - 1, cap, half_d), BF16),
            pltpu.VMEM((cap, out_w), BF16),
            pltpu.VMEM((cap, out_w), BF16),
            pltpu.SemaphoreType.DMA((8,)),
            pltpu.SemaphoreType.DMA((n_sem,)),
            pltpu.SemaphoreType.DMA((n_sem,)),
        ],
        compiler_params=pltpu.CompilerParams(
            collective_id=0, has_side_effects=True, vmem_limit_bytes=60 * 1024 * 1024
        ),
    )(
        tokens,
        light_in,
        light_out,
        heavy_in,
        heavy_out,
        route_index,
        route_count,
        route_gate,
        cotangent,
    )
    tile = tile_of(width, 512)
    grad_in, grad_out = pl.pallas_call(
        grad_kernel,
        grid=(width // tile,),
        out_shape=(
            jax.ShapeDtypeStruct((width, ffh), BF16),
            jax.ShapeDtypeStruct((ffh, width), BF16),
        ),
        in_specs=[
            pl.BlockSpec((2, total_rows, tile), lambda i: (0, 0, i)),
            pl.BlockSpec((total_rows, ffh), lambda i: (0, 0)),
            pl.BlockSpec((total_rows, ffh), lambda i: (0, 0)),
        ],
        out_specs=(
            pl.BlockSpec((tile, ffh), lambda i: (i, 0)),
            pl.BlockSpec((ffh, tile), lambda i: (0, i)),
        ),
        compiler_params=pltpu.CompilerParams(vmem_limit_bytes=60 * 1024 * 1024),
    )(rows, hidden, slope)
    return mixed, grad_in, grad_out


def solution(mesh):
    in_specs = (
        P("seq", "mp"),
        P(None, ("branch", "mp")),
        P(("branch", "mp"), None),
        P(None, ("branch", "seq", "mp")),
        P(("branch", "seq", "mp"), None),
        P("seq", None),
        P("seq"),
        P("seq", None),
        P("seq", "mp"),
    )
    out_specs = (
        P("seq", ("branch", "mp")),
        P(None, ("branch", "seq", "mp")),
        P(("branch", "seq", "mp"), None),
    )
    return jax.shard_map(
        functools.partial(per_device, mesh.shape["seq"]),
        mesh=mesh,
        in_specs=in_specs,
        out_specs=out_specs,
        check_vma=False,
    )
```
